32 devices in a mesh: groups: 2 (over y), tile: 4 (over z), pair: 2 (over x), sub: 2 (over core).
Axes of the slice: x: 2, y: 2, z: 4, core: 2. Of those that a mesh axis runs over, the one named last changes fastest.
Arguments:
- ref_chips: bfloat16 [4, 256, 4096], P(('groups', 'pair'), ('tile', 'sub')), parts along dimension 0, may hold values from -300 to 700
- search_windows: bfloat16 [4, 512, 16384], P(('groups', 'pair'), ('tile', 'sub')), parts along dimension 0, may hold values from -300 to 700
- dest_block: int32 [4, 512, 1], P(('groups', 'pair'), ('tile', 'sub')), parts along dimension 0, may hold values from 0 to 7; in each aligned block of 64 rows (0 to 63, 64 to 127, ..., all dimensions but the last counted through in order) at most 16 rows name the same one
- dest_slot: int32 [4, 512], P(('groups', 'pair'), ('tile', 'sub')), parts along dimension 0, may hold values from 0 to 31
Outputs:
- smoothed_scores: float32 [4, 256, 4096], P(('groups', 'pair'), ('tile', 'sub')), parts along dimension 0
The draws below stay inside these ranges and needn't reach their ends.
There are 2 independent parts, one for each index of `groups`. The reference program is written for one: setup_inputs(seed, part) draws one part's arguments, and reference() takes and returns one part's arrays. A program takes and returns all parts, laid end to end along the dimension named above; each array names one. Nothing has to cross between parts.
Inputs may be any that keep to these rules, and one draw needn't show every extreme that they name: `dest_block`: in the rows of one device (aligned blocks of 64 windows), no block index is named by more than 16 windows.
All inputs are finite; a program needn't handle non-finite values.
Results may differ from the reference program's by a relative error of at most 0.0003.
Values may be sent and summed in bfloat16 or wider, within the bound.
A program may use at most 64 MiB of HBM per device.

```python
import math
import jax
import jax.numpy as jnp
import numpy as np
from jax import lax

CHIP = 64
WIN = 128
OFF = 64
GC = 8
W_DEV = 64
CAP = 16
CHIP_DEV = 32
NCHIP = 256
ROWS = 32
NWIN = 512
PAIRS = 2
N_TILE = 4
N_SUB = 2


def textured(key, leading, side_length):
    parts_keys = jax.random.split(key, 3)
    noise = jax.random.truncated_normal(parts_keys[0], -4.0, 4.0, leading + (side_length, side_length), jnp.float32)
    spread = math.log(10.0)
    row_scale = jnp.exp(spread * jax.random.uniform(parts_keys[1], leading + (side_length, 1), jnp.float32))
    column_scale = jnp.exp(spread * jax.random.uniform(parts_keys[2], leading + (1, side_length), jnp.float32))
    values = row_scale * column_scale * (1.0 + noise)
    return values.reshape(leading + (side_length * side_length,))


def draw_ref_chips(key, part):
    return textured(jax.random.fold_in(key, 101), (PAIRS, NCHIP), CHIP).astype(jnp.bfloat16)


def draw_search_windows(key, part):
    return textured(jax.random.fold_in(key, 202), (PAIRS, NWIN), WIN).astype(jnp.bfloat16)


def plant(values, rng, smallest, largest):
    shape = values.shape
    place = [jax.random.randint(jax.random.fold_in(rng, axis), (), 0, shape[axis]) for axis in range(len(shape))]
    values = values.at[tuple(place)].set(smallest)
    longest = shape.index(max(shape))
    place[longest] = (place[longest] + 1) % shape[longest]
    return values.at[tuple(place)].set(largest)


def deal_out(rng, own, number, rows, number_of, top, most, lean):
    order = jax.random.permutation(rng, number_of)
    crowded, usual = load_shares(number_of, rows * top, most, lean, True), load_shares(number_of, rows * top, most, lean, False)
    places = jnp.arange(number_of)

    def named(lengths, offset_by):
        used = int((lengths > 0).sum())
        fixed = max(1, used // 4)
        moved = fixed + (places - fixed + offset_by * (used - fixed)) % max(1, number_of - fixed)
        return jnp.zeros((number_of,), jnp.int32).at[order[jnp.where(places < fixed, places, moved)]].set(jnp.asarray(lengths, jnp.int32))

    lengths = jnp.where(number % 4 == 0, named(crowded, number // 4), named(usual, number - number // 4 - 1))
    mixed = jax.random.permutation(jax.random.fold_in(own, 3), number_of)
    donor, taker = mixed[0:number_of // 2 * 2:2], mixed[1:number_of // 2 * 2:2]
    slack = jnp.minimum(lengths[donor] - 1, most - lengths[taker]) // 2
    slack = jnp.where((donor == order[0]) | (taker == order[0]) | (lengths[taker] == 0), 0, jnp.maximum(slack, 0))
    moved = jax.random.randint(jax.random.fold_in(own, 4), (number_of // 2,), 0, 1 << 20) % (slack + 1)
    lengths = lengths.at[donor].add(-moved).at[taker].add(moved)
    items = jnp.searchsorted(jnp.cumsum(lengths), jnp.arange(rows * top), side="right").astype(jnp.int32)
    listing = items.reshape(top, rows).T
    listing = listing[jax.random.permutation(jax.random.fold_in(own, 1), rows)]
    offset_by = jax.random.randint(jax.random.fold_in(own, 2), (rows, 1), 0, top)
    return jnp.take_along_axis(listing, (jnp.arange(top)[None, :] + offset_by) % top, axis=1)


def load_shares(count, total, most, lean, full):
    loads = [(1 << 20) // math.isqrt(grade ** lean) + 1 for grade in range(1, count + 1)]
    largest = most if full else min(most, max(-(-total // count), total * loads[0] // sum(loads)))
    least = 1 if total - largest >= count - 1 else 0
    given, spare = [largest] + [least] * (count - 1), total - largest - least * (count - 1)
    while spare > 0:
        free = [i for i in range(1, count) if given[i] < largest] or [i for i in range(1, count) if given[i] < most]
        whole, left = sum([loads[i] for i in free]), spare
        for i in free:
            extra = min(most - given[i], max(1, left * loads[i] // whole), spare)
            given[i] = given[i] + extra
            spare = spare - extra
    return np.array(given)


def setup_inputs(seed: int = 0, part: int = 0) -> dict:
    streams_of = jax.random.split(jax.random.key(seed), 5)
    own_keys = jax.random.split(jax.random.fold_in(streams_of[4], part), 5)
    ref_chips = draw_ref_chips(jax.random.fold_in(jax.random.fold_in(streams_of[4], part), 71), part)
    search_windows = draw_search_windows(jax.random.fold_in(jax.random.fold_in(streams_of[4], part), 71), part)
    dest_block_keys = jax.random.split(jax.random.fold_in(own_keys[2], 1), PAIRS * NWIN // W_DEV)
    dest_block_turns = jax.random.permutation(jax.random.fold_in(own_keys[2], 3), PAIRS * NWIN // W_DEV)
    dest_block = jax.vmap(lambda own, number: deal_out(jax.random.fold_in(own_keys[2], 2), own, number, W_DEV, N_TILE * N_SUB, 1, CAP, 2))(dest_block_keys, dest_block_turns).reshape((PAIRS, NWIN, 1))
    dest_slot = plant(jax.random.randint(own_keys[3], (PAIRS, NWIN), 0, CHIP_DEV), jax.random.fold_in(own_keys[3], 1), 0, CHIP_DEV - 1).astype(jnp.int32)
    return dict(ref_chips=ref_chips, search_windows=search_windows, dest_block=dest_block, dest_slot=dest_slot)


def reference(ref_chips, search_windows, dest_block, dest_slot):

    def one_pair(operands):
        chips_raw, windows_raw, blocks, slots = operands
        chip_float = chips_raw.astype(jnp.float32).reshape(NCHIP, CHIP, CHIP)
        centred = chip_float - lax.optimization_barrier(jnp.mean(chip_float, axis=(1, 2), keepdims=True))
        chip_std = jnp.sqrt(lax.optimization_barrier(jnp.mean(centred * centred, axis=(1, 2))) + 1e-06)
        targets = (blocks[:, 0] * CHIP_DEV + slots).astype(jnp.int32)
        window_float = windows_raw.astype(jnp.float32).reshape(NWIN, WIN, WIN)
        padded = jnp.pad(centred[targets], ((0, 0), (0, WIN - CHIP), (0, WIN - CHIP)))
        cross = jnp.fft.irfft2(jnp.conj(jnp.fft.rfft2(padded)) * jnp.fft.rfft2(window_float), s=(WIN, WIN))
        numerator = cross[:, :OFF, :OFF]
        starts = jnp.arange(OFF, dtype=jnp.int32)[:, None]
        pixels = jnp.arange(WIN, dtype=jnp.int32)[None, :]
        window_band = ((pixels >= starts) & (pixels < starts + CHIP)).astype(jnp.float32)
        first_sum = jnp.einsum('ax,wxy,ey->wae', window_band, window_float, window_band, precision=lax.Precision.HIGHEST)
        second_sum = jnp.einsum('ax,wxy,ey->wae', window_band, window_float * window_float, window_band, precision=lax.Precision.HIGHEST)
        patch_mean = first_sum / (CHIP * CHIP)
        patch_var = second_sum / (CHIP * CHIP) - patch_mean * patch_mean
        score = numerator / (CHIP * chip_std[targets][:, None, None] * jnp.sqrt(patch_var + 1e-06))
        total = jax.ops.segment_sum(score.reshape(NWIN, OFF * OFF), targets, num_segments=NCHIP)
        looks = jax.ops.segment_sum(jnp.ones((NWIN,), jnp.float32), targets, num_segments=NCHIP)
        average = total / jnp.maximum(looks, 1.0)[:, None]
        grid = average.reshape(ROWS, GC, OFF * OFF)
        edges = jnp.pad(grid, ((1, 1), (1, 1), (0, 0)))
        smoothed = (4.0 * grid + edges[:-2, 1:-1] + edges[2:, 1:-1] + edges[1:-1, :-2] + edges[1:-1, 2:]) / 8.0
        return smoothed.reshape(NCHIP, OFF * OFF)
    return lax.map(one_pair, (ref_chips, search_windows, dest_block, dest_slot))
```

```python
import functools

import jax
import jax.numpy as jnp
from jax import lax
from jax.experimental import pallas as pl
from jax.experimental.pallas import tpu as pltpu
from jax.sharding import PartitionSpec as P

CHIP = 64
WIN = 128
GC = 8
LANES = 128
SUBLANES = 8
PHASES = 4
DEPTH = 80
EACH = 2

epsilon = 1e-06


def padded(block, sides, width):
    for axis, dim in sides:
        count = lax.axis_size(axis)
        forward = [(i, i + 1) for i in range(count - 1)]
        backward = [(target, source) for source, target in forward]
        low = lax.ppermute(
            lax.slice_in_dim(block, block.shape[dim] - width, None, axis=dim), axis, forward
        )
        high = lax.ppermute(lax.slice_in_dim(block, 0, width, axis=dim), axis, backward)
        block = jnp.concatenate([low, block, high], axis=dim)
    return block


def box_sums(image):
    step = 1
    while step < CHIP:
        image = image + pltpu.roll(image, WIN - step, 0)
        step *= 2
    image = image[:CHIP]
    step = 1
    while step < CHIP:
        image = image + pltpu.roll(image, WIN - step, 1)
        step *= 2
    return image


def correlate(chip_ref, window_ref, even_ref, odd_ref):
    chip = chip_ref.astype(jnp.float32)
    total = jnp.sum(jnp.sum(chip, axis=0, keepdims=True), axis=1, keepdims=True)
    mean = total / (CHIP * CHIP)
    centred = chip - mean
    square = jnp.sum(jnp.sum(centred * centred, axis=0, keepdims=True), axis=1, keepdims=True)
    chip_std = jnp.sqrt(square / (CHIP * CHIP) + epsilon)

    wide = jnp.concatenate([chip, jnp.zeros((CHIP, LANES - CHIP), jnp.float32)], axis=1)
    left = []
    for phase in range(PHASES):
        rows = []
        for v in range(phase, CHIP, PHASES):
            row = jnp.broadcast_to(wide[v : v + 1], (SUBLANES, LANES))
            rows.append(pltpu.roll(row, 0, 1, stride=1, stride_axis=0))
        left.append(jnp.concatenate(rows, axis=0).astype(jnp.bfloat16)[:, :DEPTH])
    left = jnp.concatenate(left, axis=1)

    window = window_ref.astype(jnp.float32)
    for phase in range(PHASES):
        moved = window if phase == 0 else pltpu.roll(window, WIN - phase, 1)
        even_ref[phase] = moved.astype(jnp.bfloat16)
        odd_ref[phase] = pltpu.roll(moved, WIN - SUBLANES, 0).astype(jnp.bfloat16)

    groups = CHIP // SUBLANES
    surfaces = []
    for pair in range(groups // 2):
        start = 2 * SUBLANES * pair
        right = jnp.concatenate(
            [
                jnp.concatenate([ref[phase, start : start + DEPTH] for phase in range(PHASES)], axis=0)
                for ref in (even_ref, odd_ref)
            ],
            axis=1,
        )
        partial = jnp.dot(left, right, preferred_element_type=jnp.float32)
        for half in range(2):
            part = partial[:, half * LANES : (half + 1) * LANES]
            value = part[:SUBLANES]
            for far in range(1, CHIP // PHASES):
                rows = part[far * SUBLANES : (far + 1) * SUBLANES]
                value = value + pltpu.roll(rows, LANES - PHASES * far, 1)
            surfaces.append(value)
    raw = jnp.concatenate(surfaces, axis=0)

    first = box_sums(window)
    second = box_sums(window * window)
    patch_mean = first / (CHIP * CHIP)
    patch_var = second / (CHIP * CHIP) - patch_mean * patch_mean
    numerator = raw - mean * first
    return numerator / (CHIP * chip_std * jnp.sqrt(patch_var + epsilon))


def match_kernel(places_ref, chips_ref, windows_ref, out_ref, even_ref, odd_ref):
    step = pl.program_id(0)

    @pl.when(step == 0)
    def _():
        out_ref[...] = jnp.zeros_like(out_ref)

    for item in range(EACH):
        score = correlate(chips_ref[item], windows_ref[item], even_ref.at[item], odd_ref.at[item])
        half = CHIP // 2
        low, high = score[:half], pltpu.roll(score[half:], CHIP, 1)
        lane = lax.broadcasted_iota(jnp.int32, (half, LANES), 1)
        out_ref[places_ref[step * EACH + item]] = jnp.where(lane < CHIP, low, high)


def match(positions, chips, windows, slot_amount):
    amount = windows.shape[0]
    half = CHIP // 2
    return pl.pallas_call(
        match_kernel,
        out_shape=jax.ShapeDtypeStruct((slot_amount, half, LANES), jnp.float32),
        grid_spec=pltpu.PrefetchScalarGridSpec(
            num_scalar_prefetch=1,
            grid=(amount // EACH,),
            in_specs=[
                pl.BlockSpec((EACH, CHIP, CHIP), lambda i, p: (i, 0, 0)),
                pl.BlockSpec((EACH, WIN, WIN), lambda i, p: (i, 0, 0)),
            ],
            out_specs=pl.BlockSpec((slot_amount, half, LANES), lambda i, p: (0, 0, 0)),
            scratch_shapes=[
                pltpu.VMEM((EACH, PHASES, WIN, LANES), jnp.bfloat16),
                pltpu.VMEM((EACH, PHASES, WIN, LANES), jnp.bfloat16),
            ],
        ),
        compiler_params=pltpu.CompilerParams(vmem_limit_bytes=40 * 1024 * 1024),
        cost_estimate=pl.CostEstimate(
            flops=amount * 2 * 128 * 512 * 1024, bytes_accessed=8 * 1024 * 1024, transcendentals=0
        ),
    )(positions, chips, windows)


def on_device(ref_chips, search_windows, dest_block, dest_slot):
    axes = ("tile", "sub")
    chips = ref_chips[0]
    windows = search_windows[0]
    targets = dest_block[0, :, 0]
    target_slot = dest_slot[0]
    window_amount = windows.shape[0]
    chip_amount = chips.shape[0]
    devices = lax.axis_size(axes)
    capacity = max(2, 2 * window_amount // devices)
    slot_amount = devices * capacity
    order = jnp.arange(window_amount, dtype=jnp.int32)
    matches = targets[:, None] == targets[None, :]
    earlier = order[:, None] > order[None, :]
    ranking = jnp.sum((matches & earlier).astype(jnp.int32), axis=1)
    positions = targets * capacity + ranking

    turned = jnp.swapaxes(chips.reshape(chip_amount, CHIP, CHIP), 1, 2).reshape(chip_amount, -1)
    everyone = lax.all_gather(turned, axes, axis=0, tiled=True)
    own_chips = jnp.take(everyone, targets * chip_amount + target_slot, axis=0)

    slots = jnp.arange(slot_amount, dtype=jnp.int32)
    slot_buffer = jnp.max(
        jnp.where(positions[None, :] == slots[:, None], target_slot[None, :], -1), axis=1
    )
    slots_here = lax.all_to_all(slot_buffer, axes, split_axis=0, concat_axis=0, tiled=True)

    score_buffer = match(
        positions,
        own_chips.reshape(window_amount, CHIP, CHIP),
        windows.reshape(window_amount, WIN, WIN),
        slot_amount,
    )
    scores = lax.all_to_all(score_buffer, axes, split_axis=0, concat_axis=0, tiled=True)
    scores = scores.reshape(slot_amount, CHIP * CHIP)
    hits_table = (slots_here[None, :] == jnp.arange(chip_amount, dtype=jnp.int32)[:, None]).astype(
        jnp.float32
    )
    total = jnp.dot(hits_table, scores, precision=lax.Precision.HIGHEST)
    looks = jnp.sum(hits_table, axis=1)
    average = total / jnp.maximum(looks, 1.0)[:, None]
    grid = average.reshape(-1, GC, CHIP * CHIP)
    extended = padded(grid, ((axes, 0),), 1)
    vertical = extended[:-2] + extended[2:]
    sideways = jnp.pad(grid, ((0, 0), (1, 1), (0, 0)))
    horizontal = sideways[:, :-2] + sideways[:, 2:]
    smoothed = (4.0 * grid + vertical + horizontal) / 8.0
    smoothed = smoothed.reshape(chip_amount, CHIP // 2, 2, CHIP)
    return jnp.swapaxes(smoothed, 1, 2).reshape(1, chip_amount, CHIP * CHIP)


def solution(mesh):
    return jax.shard_map(
        on_device,
        mesh=mesh,
        in_specs=(
            P(("groups", "pair"), ("tile", "sub"), None),
            P(("groups", "pair"), ("tile", "sub"), None),
            P(("groups", "pair"), ("tile", "sub"), None),
            P(("groups", "pair"), ("tile", "sub")),
        ),
        out_specs=P(("groups", "pair"), ("tile", "sub"), None),
        check_vma=False,
    )
```

```python
import functools

import jax
import jax.numpy as jnp
from jax import lax
from jax.experimental import pallas as pl
from jax.experimental.pallas import tpu as pltpu
from jax.sharding import PartitionSpec as P

CHIP = 64
WIN = 128
GC = 8
LANES = 128
SUBLANES = 8
PHASES = 4
DEPTH = 80
EACH = 2

epsilon = 1e-06


def padded(block, sides, width):
    for axis, dim in sides:
        count = lax.axis_size(axis)
        forward = [(i, i + 1) for i in range(count - 1)]
        backward = [(target, source) for source, target in forward]
        low = lax.ppermute(
            lax.slice_in_dim(block, block.shape[dim] - width, None, axis=dim), axis, forward
        )
        high = lax.ppermute(lax.slice_in_dim(block, 0, width, axis=dim), axis, backward)
        block = jnp.concatenate([low, block, high], axis=dim)
    return block


def box_sums(image):
    step = 1
    while step < CHIP:
        image = image + pltpu.roll(image, WIN - step, 0)
        step *= 2
    image = image[:CHIP]
    step = 1
    while step < CHIP:
        image = image + pltpu.roll(image, WIN - step, 1)
        step *= 2
    return image


def patch_kernel(windows_ref, first_ref, inverse_ref):
    for item in range(windows_ref.shape[0]):
        window = windows_ref[item].astype(jnp.float32)
        first = box_sums(window)
        second = box_sums(window * window)
        patch_mean = first / (CHIP * CHIP)
        patch_var = second / (CHIP * CHIP) - patch_mean * patch_mean
        first_ref[item] = first
        inverse_ref[item] = 1.0 / (CHIP * jnp.sqrt(patch_var + epsilon))


def patches(windows):
    amount = windows.shape[0]
    surface = jax.ShapeDtypeStruct((amount, CHIP, LANES), jnp.float32)
    block = pl.BlockSpec((EACH, CHIP, LANES), lambda i: (i, 0, 0))
    return pl.pallas_call(
        patch_kernel,
        out_shape=(surface, surface),
        grid=(amount // EACH,),
        in_specs=[pl.BlockSpec((EACH, WIN, WIN), lambda i: (i, 0, 0))],
        out_specs=(block, block),
        cost_estimate=pl.CostEstimate(
            flops=amount * 2 * 128 * 512 * 256, bytes_accessed=40 * 1024 * 1024, transcendentals=0
        ),
    )(windows)


def correlate(chip_ref, window_ref, first_ref, inverse_ref, even_ref, odd_ref):
    half = CHIP // 2
    chip = chip_ref[...].astype(jnp.float32)
    total = jnp.sum(jnp.sum(chip, axis=0, keepdims=True), axis=1, keepdims=True)
    mean = total / (CHIP * CHIP)
    centred = chip - mean
    square = jnp.sum(jnp.sum(centred * centred, axis=0, keepdims=True), axis=1, keepdims=True)
    chip_std = jnp.sqrt(square / (CHIP * CHIP) + epsilon)

    lane = lax.broadcasted_iota(jnp.int32, (half, LANES), 1)
    wide = (jnp.where(lane < CHIP, chip, 0.0), jnp.where(lane < CHIP, pltpu.roll(chip, CHIP, 1), 0.0))
    left = []
    for phase in range(PHASES):
        rows = []
        for v in range(phase, CHIP, PHASES):
            row = wide[v // half][v % half : v % half + 1]
            row = jnp.broadcast_to(row, (SUBLANES, LANES))
            rows.append(pltpu.roll(row, 0, 1, stride=1, stride_axis=0))
        left.append(jnp.concatenate(rows, axis=0).astype(jnp.bfloat16)[:, :DEPTH])
    left = jnp.concatenate(left, axis=1)

    window = window_ref[...].astype(jnp.float32)
    for phase in range(PHASES):
        moved = window if phase == 0 else pltpu.roll(window, WIN - phase, 1)
        even_ref[phase] = moved.astype(jnp.bfloat16)
        odd_ref[phase] = pltpu.roll(moved, WIN - SUBLANES, 0).astype(jnp.bfloat16)

    groups = CHIP // SUBLANES
    surfaces = []
    for pair in range(groups // 2):
        start = 2 * SUBLANES * pair
        right = jnp.concatenate(
            [
                jnp.concatenate([ref[phase, start : start + DEPTH] for phase in range(PHASES)], axis=0)
                for ref in (even_ref, odd_ref)
            ],
            axis=1,
        )
        partial = jnp.dot(left, right, preferred_element_type=jnp.float32)
        for side in range(2):
            part = partial[:, side * LANES : (side + 1) * LANES]
            value = part[:SUBLANES]
            for far in range(1, CHIP // PHASES):
                rows = part[far * SUBLANES : (far + 1) * SUBLANES]
                value = value + pltpu.roll(rows, LANES - PHASES * far, 1)
            surfaces.append(value)
    raw = jnp.concatenate(surfaces, axis=0)
    return (raw - mean * first_ref[...]) * (inverse_ref[...] / chip_std)


def match_kernel(places_ref, names_ref, *refs):
    chips, rest = refs[:EACH], refs[EACH:]
    windows_ref, first_ref, inverse_ref, out_ref, scale_ref, even_ref, odd_ref = rest
    step = pl.program_id(0)

    @pl.when(step == 0)
    def _():
        out_ref[...] = jnp.zeros_like(out_ref)
        scale_ref[...] = jnp.zeros_like(scale_ref)

    half = CHIP // 2
    lane = lax.broadcasted_iota(jnp.int32, (half, LANES), 1)
    for item in range(EACH):
        score = correlate(
            chips[item].at[0],
            windows_ref.at[item],
            first_ref.at[item],
            inverse_ref.at[item],
            even_ref.at[item],
            odd_ref.at[item],
        )
        low, high = score[:half], pltpu.roll(score[half:], CHIP, 1)
        packed = jnp.where(lane < CHIP, low, high)
        size = jnp.abs(packed)
        largest = jnp.max(jnp.max(size, axis=0, keepdims=True), axis=1, keepdims=True)
        largest = jnp.maximum(largest, 1e-30)
        code = jnp.sqrt(size * (1.0 / largest)) * 32767.0
        code = jnp.minimum(code + 0.5, 32767.0).astype(jnp.int32)
        code = jnp.where(packed < 0, -code, code)
        place = places_ref[step * EACH + item]
        out_ref[place] = code.astype(jnp.int16)
        scale_ref[place] = jnp.broadcast_to(largest, (SUBLANES, LANES))


def match(positions, names, everyone, windows, first, inverse, slot_amount):
    amount = windows.shape[0]
    half = CHIP // 2

    def chip_spec(item):
        return pl.BlockSpec((1, half, LANES), lambda i, p, n: (n[i * EACH + item], 0, 0))

    surface = pl.BlockSpec((EACH, CHIP, LANES), lambda i, p, n: (i, 0, 0))
    return pl.pallas_call(
        match_kernel,
        out_shape=(
            jax.ShapeDtypeStruct((slot_amount, half, LANES), jnp.int16),
            jax.ShapeDtypeStruct((slot_amount, SUBLANES, LANES), jnp.float32),
        ),
        grid_spec=pltpu.PrefetchScalarGridSpec(
            num_scalar_prefetch=2,
            grid=(amount // EACH,),
            in_specs=[chip_spec(item) for item in range(EACH)]
            + [pl.BlockSpec((EACH, WIN, WIN), lambda i, p, n: (i, 0, 0)), surface, surface],
            out_specs=(
                pl.BlockSpec((slot_amount, half, LANES), lambda i, p, n: (0, 0, 0)),
                pl.BlockSpec((slot_amount, SUBLANES, LANES), lambda i, p, n: (0, 0, 0)),
            ),
            scratch_shapes=[
                pltpu.VMEM((EACH, PHASES, WIN, LANES), jnp.bfloat16),
                pltpu.VMEM((EACH, PHASES, WIN, LANES), jnp.bfloat16),
            ],
        ),
        compiler_params=pltpu.CompilerParams(vmem_limit_bytes=40 * 1024 * 1024),
        cost_estimate=pl.CostEstimate(
            flops=amount * 2 * 128 * 512 * 1024, bytes_accessed=8 * 1024 * 1024, transcendentals=0
        ),
    )(positions, names, *([everyone] * EACH), windows, first, inverse)


def on_device(ref_chips, search_windows, dest_block, dest_slot):
    axes = ("tile", "sub")
    chips = ref_chips[0]
    windows = search_windows[0]
    targets = dest_block[0, :, 0]
    target_slot = dest_slot[0]
    window_amount = windows.shape[0]
    chip_amount = chips.shape[0]
    half = CHIP // 2
    devices = lax.axis_size(axes)
    capacity = max(2, 2 * window_amount // devices)
    slot_amount = devices * capacity

    turned = jnp.swapaxes(chips.reshape(chip_amount, CHIP, CHIP), 1, 2)
    turned = jnp.swapaxes(turned.reshape(chip_amount, 2, half, CHIP), 1, 2)
    everyone = lax.all_gather(turned.reshape(chip_amount, half, LANES), axes, axis=0, tiled=True)

    order = jnp.arange(window_amount, dtype=jnp.int32)
    matches = targets[:, None] == targets[None, :]
    earlier = order[:, None] > order[None, :]
    ranking = jnp.sum((matches & earlier).astype(jnp.int32), axis=1)
    positions = targets * capacity + ranking
    slots = jnp.arange(slot_amount, dtype=jnp.int32)
    slot_buffer = jnp.max(
        jnp.where(positions[None, :] == slots[:, None], target_slot[None, :], -1), axis=1
    )

    windows = windows.reshape(window_amount, WIN, WIN)
    first, inverse = patches(windows)
    codes, scales = match(
        positions,
        targets * chip_amount + target_slot,
        everyone,
        windows,
        first,
        inverse,
        slot_amount,
    )
    codes = lax.all_to_all(codes, axes, split_axis=0, concat_axis=0, tiled=True)
    notes = jnp.concatenate([scales[:, 0, 0], slot_buffer.astype(jnp.float32)])
    notes = lax.all_gather(notes, axes, axis=0).reshape(devices, 2, devices, capacity)
    notes = lax.dynamic_index_in_dim(notes, lax.axis_index(axes), 2, keepdims=False)
    notes = notes.transpose(0, 2, 1).reshape(slot_amount, 2)
    codes = codes.astype(jnp.float32) * (1.0 / 32767.0)
    scores = (codes * jnp.abs(codes)).reshape(slot_amount, CHIP * CHIP)
    hits_table = (
        notes[None, :, 1] == jnp.arange(chip_amount, dtype=jnp.float32)[:, None]
    ).astype(jnp.float32)
    looks = jnp.sum(hits_table, axis=1)
    share = hits_table * notes[None, :, 0] / jnp.maximum(looks, 1.0)[:, None]
    average = jnp.dot(share, scores, precision=lax.Precision.HIGHEST)
    grid = average.reshape(-1, GC, CHIP * CHIP)
    extended = padded(grid, ((axes, 0),), 1)
    vertical = extended[:-2] + extended[2:]
    sideways = jnp.pad(grid, ((0, 0), (1, 1), (0, 0)))
    horizontal = sideways[:, :-2] + sideways[:, 2:]
    smoothed = (4.0 * grid + vertical + horizontal) / 8.0
    smoothed = smoothed.reshape(chip_amount, half, 2, CHIP)
    return jnp.swapaxes(smoothed, 1, 2).reshape(1, chip_amount, CHIP * CHIP)


def solution(mesh):
    return jax.shard_map(
        on_device,
        mesh=mesh,
        in_specs=(
            P(("groups", "pair"), ("tile", "sub"), None),
            P(("groups", "pair"), ("tile", "sub"), None),
            P(("groups", "pair"), ("tile", "sub"), None),
            P(("groups", "pair"), ("tile", "sub")),
        ),
        out_specs=P(("groups", "pair"), ("tile", "sub"), None),
        check_vma=False,
    )
```

```python
import functools

import jax
import jax.numpy as jnp
from jax import lax
from jax.experimental import pallas as pl
from jax.experimental.pallas import tpu as pltpu
from jax.sharding import PartitionSpec as P

CHIP = 64
WIN = 128
GC = 8
LANES = 128
SUBLANES = 8
PHASES = 4
GROUP = 16
DEPTH = CHIP + GROUP
EACH = 4

epsilon = 1e-06


def padded(block, sides, width):
    for axis, dim in sides:
        count = lax.axis_size(axis)
        forward = [(i, i + 1) for i in range(count - 1)]
        backward = [(target, source) for source, target in forward]
        low = lax.ppermute(
            lax.slice_in_dim(block, block.shape[dim] - width, None, axis=dim), axis, forward
        )
        high = lax.ppermute(lax.slice_in_dim(block, 0, width, axis=dim), axis, backward)
        block = jnp.concatenate([low, block, high], axis=dim)
    return block


def box_sums(image):
    step = 1
    while step < CHIP:
        image = image + pltpu.roll(image, WIN - step, 0)
        step *= 2
    image = image[:CHIP]
    step = 1
    while step < CHIP:
        image = image + pltpu.roll(image, WIN - step, 1)
        step *= 2
    return image


def patch_kernel(windows_ref, first_ref, inverse_ref):
    for item in range(windows_ref.shape[0]):
        window = windows_ref[item].astype(jnp.float32)
        first = box_sums(window)
        second = box_sums(window * window)
        patch_mean = first / (CHIP * CHIP)
        patch_var = second / (CHIP * CHIP) - patch_mean * patch_mean
        first_ref[item] = first
        inverse_ref[item] = 1.0 / (CHIP * jnp.sqrt(patch_var + epsilon))


def patches(windows):
    amount = windows.shape[0]
    surface = jax.ShapeDtypeStruct((amount, CHIP, LANES), jnp.float32)
    block = pl.BlockSpec((EACH, CHIP, LANES), lambda i: (i, 0, 0))
    return pl.pallas_call(
        patch_kernel,
        out_shape=(surface, surface),
        grid=(amount // EACH,),
        in_specs=[pl.BlockSpec((EACH, WIN, WIN), lambda i: (i, 0, 0))],
        out_specs=(block, block),
        cost_estimate=pl.CostEstimate(
            flops=amount * 2 * 128 * 512 * 256, bytes_accessed=40 * 1024 * 1024, transcendentals=0
        ),
    )(windows)


def correlate(chip_ref, window_ref, first_ref, inverse_ref, copies_ref):
    half = CHIP // 2
    chip = chip_ref[...].astype(jnp.float32)
    total = jnp.sum(jnp.sum(chip, axis=0, keepdims=True), axis=1, keepdims=True)
    mean = total / (CHIP * CHIP)
    centred = chip - mean
    square = jnp.sum(jnp.sum(centred * centred, axis=0, keepdims=True), axis=1, keepdims=True)
    chip_std = jnp.sqrt(square / (CHIP * CHIP) + epsilon)

    lane = lax.broadcasted_iota(jnp.int32, (half, LANES), 1)
    wide = (jnp.where(lane < CHIP, chip, 0.0), jnp.where(lane < CHIP, pltpu.roll(chip, CHIP, 1), 0.0))
    left = []
    for phase in range(PHASES):
        rows = []
        for v in range(phase, CHIP, PHASES):
            row = wide[v // half][v % half : v % half + 1]
            row = jnp.broadcast_to(row, (SUBLANES, LANES))
            row = pltpu.roll(row, 0, 1, stride=1, stride_axis=0)
            rows += [row, pltpu.roll(row, SUBLANES, 1)]
        left.append(jnp.concatenate(rows, axis=0).astype(jnp.bfloat16)[:, :DEPTH])
    left = jnp.concatenate(left, axis=1)

    window = window_ref[...].astype(jnp.float32)
    for phase in range(PHASES):
        moved = window if phase == 0 else pltpu.roll(window, WIN - phase, 1)
        copies_ref[phase] = moved.astype(jnp.bfloat16)

    groups = CHIP // GROUP
    surfaces = []
    for pair in range(groups // 2):
        starts = (2 * GROUP * pair, 2 * GROUP * pair + GROUP)
        right = jnp.concatenate(
            [
                jnp.concatenate(
                    [copies_ref[phase, start : start + DEPTH] for phase in range(PHASES)], axis=0
                )
                for start in starts
            ],
            axis=1,
        )
        partial = jnp.dot(left, right, preferred_element_type=jnp.float32)
        for side in range(2):
            part = partial[:, side * LANES : (side + 1) * LANES]
            value = part[:GROUP]
            for far in range(1, CHIP // PHASES):
                rows = part[far * GROUP : (far + 1) * GROUP]
                value = value + pltpu.roll(rows, LANES - PHASES * far, 1)
            surfaces.append(value)
    raw = jnp.concatenate(surfaces, axis=0)
    return (raw - mean * first_ref[...]) * (inverse_ref[...] / chip_std)


def match_kernel(places_ref, names_ref, *refs):
    chips, rest = refs[:EACH], refs[EACH:]
    windows_ref, first_ref, inverse_ref, out_ref, scale_ref, copies_ref = rest
    step = pl.program_id(0)

    @pl.when(step == 0)
    def _():
        out_ref[...] = jnp.zeros_like(out_ref)
        scale_ref[...] = jnp.zeros_like(scale_ref)

    half = CHIP // 2
    lane = lax.broadcasted_iota(jnp.int32, (half, LANES), 1)
    for item in range(EACH):
        score = correlate(
            chips[item].at[0],
            windows_ref.at[item],
            first_ref.at[item],
            inverse_ref.at[item],
            copies_ref.at[item],
        )
        low, high = score[:half], pltpu.roll(score[half:], CHIP, 1)
        packed = jnp.where(lane < CHIP, low, high)
        size = jnp.abs(packed)
        largest = jnp.max(jnp.max(size, axis=0, keepdims=True), axis=1, keepdims=True)
        largest = jnp.maximum(largest, 1e-30)
        code = jnp.sqrt(size * (1.0 / largest)) * 32767.0
        code = jnp.minimum(code + 0.5, 32767.0).astype(jnp.int32)
        code = jnp.where(packed < 0, -code, code)
        place = places_ref[step * EACH + item]
        out_ref[place] = code.astype(jnp.int16)
        scale_ref[place] = jnp.broadcast_to(largest, (SUBLANES, LANES))


def match(positions, names, everyone, windows, first, inverse, slot_amount):
    amount = windows.shape[0]
    half = CHIP // 2

    def chip_spec(item):
        return pl.BlockSpec((1, half, LANES), lambda i, p, n: (n[i * EACH + item], 0, 0))

    surface = pl.BlockSpec((EACH, CHIP, LANES), lambda i, p, n: (i, 0, 0))
    return pl.pallas_call(
        match_kernel,
        out_shape=(
            jax.ShapeDtypeStruct((slot_amount, half, LANES), jnp.int16),
            jax.ShapeDtypeStruct((slot_amount, SUBLANES, LANES), jnp.float32),
        ),
        grid_spec=pltpu.PrefetchScalarGridSpec(
            num_scalar_prefetch=2,
            grid=(amount // EACH,),
            in_specs=[chip_spec(item) for item in range(EACH)]
            + [pl.BlockSpec((EACH, WIN, WIN), lambda i, p, n: (i, 0, 0)), surface, surface],
            out_specs=(
                pl.BlockSpec((slot_amount, half, LANES), lambda i, p, n: (0, 0, 0)),
                pl.BlockSpec((slot_amount, SUBLANES, LANES), lambda i, p, n: (0, 0, 0)),
            ),
            scratch_shapes=[
                pltpu.VMEM((EACH, PHASES, WIN, LANES), jnp.bfloat16),
            ],
        ),
        compiler_params=pltpu.CompilerParams(vmem_limit_bytes=58 * 1024 * 1024),
        cost_estimate=pl.CostEstimate(
            flops=amount * 2 * 128 * 512 * 1024, bytes_accessed=8 * 1024 * 1024, transcendentals=0
        ),
    )(positions, names, *([everyone] * EACH), windows, first, inverse)


def on_device(ref_chips, search_windows, dest_block, dest_slot):
    axes = ("tile", "sub")
    chips = ref_chips[0]
    windows = search_windows[0]
    targets = dest_block[0, :, 0]
    target_slot = dest_slot[0]
    window_amount = windows.shape[0]
    chip_amount = chips.shape[0]
    half = CHIP // 2
    devices = lax.axis_size(axes)
    capacity = max(2, 2 * window_amount // devices)
    slot_amount = devices * capacity

    turned = jnp.swapaxes(chips.reshape(chip_amount, CHIP, CHIP), 1, 2)
    turned = jnp.swapaxes(turned.reshape(chip_amount, 2, half, CHIP), 1, 2)
    everyone = lax.all_gather(turned.reshape(chip_amount, half, LANES), axes, axis=0, tiled=True)

    order = jnp.arange(window_amount, dtype=jnp.int32)
    matches = targets[:, None] == targets[None, :]
    earlier = order[:, None] > order[None, :]
    ranking = jnp.sum((matches & earlier).astype(jnp.int32), axis=1)
    positions = targets * capacity + ranking
    slots = jnp.arange(slot_amount, dtype=jnp.int32)
    slot_buffer = jnp.max(
        jnp.where(positions[None, :] == slots[:, None], target_slot[None, :], -1), axis=1
    )

    windows = windows.reshape(window_amount, WIN, WIN)
    first, inverse = patches(windows)
    codes, scales = match(
        positions,
        targets * chip_amount + target_slot,
        everyone,
        windows,
        first,
        inverse,
        slot_amount,
    )
    codes = lax.all_to_all(codes, axes, split_axis=0, concat_axis=0, tiled=True)
    notes = jnp.concatenate([scales[:, 0, 0], slot_buffer.astype(jnp.float32)])
    notes = lax.all_gather(notes, axes, axis=0).reshape(devices, 2, devices, capacity)
    notes = lax.dynamic_index_in_dim(notes, lax.axis_index(axes), 2, keepdims=False)
    notes = notes.transpose(0, 2, 1).reshape(slot_amount, 2)
    codes = codes.astype(jnp.float32) * (1.0 / 32767.0)
    scores = (codes * jnp.abs(codes)).reshape(slot_amount, CHIP * CHIP)
    hits_table = (
        notes[None, :, 1] == jnp.arange(chip_amount, dtype=jnp.float32)[:, None]
    ).astype(jnp.float32)
    looks = jnp.sum(hits_table, axis=1)
    share = hits_table * notes[None, :, 0] / jnp.maximum(looks, 1.0)[:, None]
    average = jnp.dot(share, scores, precision=lax.Precision.HIGHEST)
    grid = average.reshape(-1, GC, CHIP * CHIP)
    extended = padded(grid, ((axes, 0),), 1)
    vertical = extended[:-2] + extended[2:]
    sideways = jnp.pad(grid, ((0, 0), (1, 1), (0, 0)))
    horizontal = sideways[:, :-2] + sideways[:, 2:]
    smoothed = (4.0 * grid + vertical + horizontal) / 8.0
    smoothed = smoothed.reshape(chip_amount, half, 2, CHIP)
    return jnp.swapaxes(smoothed, 1, 2).reshape(1, chip_amount, CHIP * CHIP)


def solution(mesh):
    return jax.shard_map(
        on_device,
        mesh=mesh,
        in_specs=(
            P(("groups", "pair"), ("tile", "sub"), None),
            P(("groups", "pair"), ("tile", "sub"), None),
            P(("groups", "pair"), ("tile", "sub"), None),
            P(("groups", "pair"), ("tile", "sub")),
        ),
        out_specs=P(("groups", "pair"), ("tile", "sub"), None),
        check_vma=False,
    )
```

```python
import functools

import jax
import jax.numpy as jnp
from jax import lax
from jax.experimental import pallas as pl
from jax.experimental.pallas import tpu as pltpu
from jax.sharding import PartitionSpec as P

CHIP = 64
WIN = 128
GC = 8
LANES = 128
SUBLANES = 8
PHASES = 4
DEPTH = 80
EACH = 2
SUMMED = 4

epsilon = 1e-06


def padded(block, sides, width):
    for axis, dim in sides:
        count = lax.axis_size(axis)
        forward = [(i, i + 1) for i in range(count - 1)]
        backward = [(target, source) for source, target in forward]
        low = lax.ppermute(
            lax.slice_in_dim(block, block.shape[dim] - width, None, axis=dim), axis, forward
        )
        high = lax.ppermute(lax.slice_in_dim(block, 0, width, axis=dim), axis, backward)
        block = jnp.concatenate([low, block, high], axis=dim)
    return block


def box_sums(image):
    step = 1
    while step < CHIP:
        image = image + pltpu.roll(image, WIN - step, 0)
        step *= 2
    image = image[:CHIP]
    step = 1
    while step < CHIP:
        image = image + pltpu.roll(image, WIN - step, 1)
        step *= 2
    return image


def patch_kernel(windows_ref, first_ref, inverse_ref):
    for item in range(windows_ref.shape[0]):
        window = windows_ref[item].astype(jnp.float32)
        first = box_sums(window)
        second = box_sums(window * window)
        patch_mean = first / (CHIP * CHIP)
        patch_var = second / (CHIP * CHIP) - patch_mean * patch_mean
        first_ref[item] = first
        inverse_ref[item] = 1.0 / (CHIP * jnp.sqrt(patch_var + epsilon))


def patches(windows):
    amount = windows.shape[0]
    surface = jax.ShapeDtypeStruct((amount, CHIP, LANES), jnp.float32)
    block = pl.BlockSpec((SUMMED, CHIP, LANES), lambda i: (i, 0, 0))
    return pl.pallas_call(
        patch_kernel,
        out_shape=(surface, surface),
        grid=(amount // SUMMED,),
        in_specs=[pl.BlockSpec((SUMMED, WIN, WIN), lambda i: (i, 0, 0))],
        out_specs=(block, block),
        cost_estimate=pl.CostEstimate(
            flops=amount * 2 * 128 * 512 * 256, bytes_accessed=40 * 1024 * 1024, transcendentals=0
        ),
    )(windows)


def correlate(chip_ref, window_ref, first_ref, inverse_ref, even_ref, odd_ref):
    half = CHIP // 2
    chip = chip_ref[...].astype(jnp.float32)
    total = jnp.sum(jnp.sum(chip, axis=0, keepdims=True), axis=1, keepdims=True)
    mean = total / (CHIP * CHIP)
    centred = chip - mean
    square = jnp.sum(jnp.sum(centred * centred, axis=0, keepdims=True), axis=1, keepdims=True)
    chip_std = jnp.sqrt(square / (CHIP * CHIP) + epsilon)

    lane = lax.broadcasted_iota(jnp.int32, (half, LANES), 1)
    wide = (jnp.where(lane < CHIP, chip, 0.0), jnp.where(lane < CHIP, pltpu.roll(chip, CHIP, 1), 0.0))
    left = []
    for phase in range(PHASES):
        rows = []
        for v in range(phase, CHIP, PHASES):
            row = wide[v // half][v % half : v % half + 1]
            row = jnp.broadcast_to(row, (SUBLANES, LANES))
            rows.append(pltpu.roll(row, 0, 1, stride=1, stride_axis=0))
        left.append(jnp.concatenate(rows, axis=0).astype(jnp.bfloat16)[:, :DEPTH])
    left = jnp.concatenate(left, axis=1)

    window = window_ref[...].astype(jnp.float32)
    for phase in range(PHASES):
        moved = window if phase == 0 else pltpu.roll(window, WIN - phase, 1)
        even_ref[phase] = moved.astype(jnp.bfloat16)
        odd_ref[phase] = pltpu.roll(moved, WIN - SUBLANES, 0).astype(jnp.bfloat16)

    groups = CHIP // SUBLANES
    surfaces = []
    for pair in range(groups // 2):
        start = 2 * SUBLANES * pair
        right = jnp.concatenate(
            [
                jnp.concatenate([ref[phase, start : start + DEPTH] for phase in range(PHASES)], axis=0)
                for ref in (even_ref, odd_ref)
            ],
            axis=1,
        )
        partial = jnp.dot(left, right, preferred_element_type=jnp.float32)
        for side in range(2):
            part = partial[:, side * LANES : (side + 1) * LANES]
            value = part[:SUBLANES]
            for far in range(1, CHIP // PHASES):
                rows = part[far * SUBLANES : (far + 1) * SUBLANES]
                value = value + pltpu.roll(rows, LANES - PHASES * far, 1)
            surfaces.append(value)
    raw = jnp.concatenate(surfaces, axis=0)
    return (raw - mean * first_ref[...]) * (inverse_ref[...] / chip_std)


def match_kernel(places_ref, names_ref, *refs):
    chips, rest = refs[:EACH], refs[EACH:]
    windows_ref, first_ref, inverse_ref, out_ref, scale_ref, even_ref, odd_ref = rest
    step = pl.program_id(0)

    @pl.when(step == 0)
    def _():
        out_ref[...] = jnp.zeros_like(out_ref)
        scale_ref[...] = jnp.zeros_like(scale_ref)

    half = CHIP // 2
    lane = lax.broadcasted_iota(jnp.int32, (half, LANES), 1)
    for item in range(EACH):
        score = correlate(
            chips[item].at[0],
            windows_ref.at[item],
            first_ref.at[item],
            inverse_ref.at[item],
            even_ref.at[item],
            odd_ref.at[item],
        )
        low, high = score[:half], pltpu.roll(score[half:], CHIP, 1)
        packed = jnp.where(lane < CHIP, low, high)
        size = jnp.abs(packed)
        largest = jnp.max(jnp.max(size, axis=0, keepdims=True), axis=1, keepdims=True)
        largest = jnp.maximum(largest, 1e-30)
        code = jnp.sqrt(size * (1.0 / largest)) * 32767.0
        code = jnp.minimum(code + 0.5, 32767.0).astype(jnp.int32)
        code = jnp.where(packed < 0, -code, code)
        place = places_ref[step * EACH + item]
        out_ref[place] = code.astype(jnp.int16)
        scale_ref[place] = jnp.broadcast_to(largest, (SUBLANES, LANES))


def match(positions, names, everyone, windows, first, inverse, slot_amount):
    amount = windows.shape[0]
    half = CHIP // 2

    def chip_spec(item):
        return pl.BlockSpec((1, half, LANES), lambda i, p, n: (n[i * EACH + item], 0, 0))

    surface = pl.BlockSpec((EACH, CHIP, LANES), lambda i, p, n: (i, 0, 0))
    return pl.pallas_call(
        match_kernel,
        out_shape=(
            jax.ShapeDtypeStruct((slot_amount, half, LANES), jnp.int16),
            jax.ShapeDtypeStruct((slot_amount, SUBLANES, LANES), jnp.float32),
        ),
        grid_spec=pltpu.PrefetchScalarGridSpec(
            num_scalar_prefetch=2,
            grid=(amount // EACH,),
            in_specs=[chip_spec(item) for item in range(EACH)]
            + [pl.BlockSpec((EACH, WIN, WIN), lambda i, p, n: (i, 0, 0)), surface, surface],
            out_specs=(
                pl.BlockSpec((slot_amount, half, LANES), lambda i, p, n: (0, 0, 0)),
                pl.BlockSpec((slot_amount, SUBLANES, LANES), lambda i, p, n: (0, 0, 0)),
            ),
            scratch_shapes=[
                pltpu.VMEM((EACH, PHASES, WIN, LANES), jnp.bfloat16),
                pltpu.VMEM((EACH, PHASES, WIN, LANES), jnp.bfloat16),
            ],
        ),
        compiler_params=pltpu.CompilerParams(vmem_limit_bytes=58 * 1024 * 1024),
        cost_estimate=pl.CostEstimate(
            flops=amount * 2 * 128 * 512 * 1024, bytes_accessed=8 * 1024 * 1024, transcendentals=0
        ),
    )(positions, names, *([everyone] * EACH), windows, first, inverse)


def on_device(ref_chips, search_windows, dest_block, dest_slot):
    axes = ("tile", "sub")
    chips = ref_chips[0]
    windows = search_windows[0]
    targets = dest_block[0, :, 0]
    target_slot = dest_slot[0]
    window_amount = windows.shape[0]
    chip_amount = chips.shape[0]
    half = CHIP // 2
    devices = lax.axis_size(axes)
    capacity = max(2, 2 * window_amount // devices)
    slot_amount = devices * capacity

    turned = jnp.swapaxes(chips.reshape(chip_amount, CHIP, CHIP), 1, 2)
    turned = jnp.swapaxes(turned.reshape(chip_amount, 2, half, CHIP), 1, 2)
    everyone = lax.all_gather(turned.reshape(chip_amount, half, LANES), axes, axis=0, tiled=True)

    order = jnp.arange(window_amount, dtype=jnp.int32)
    matches = targets[:, None] == targets[None, :]
    earlier = order[:, None] > order[None, :]
    ranking = jnp.sum((matches & earlier).astype(jnp.int32), axis=1)
    positions = targets * capacity + ranking
    slots = jnp.arange(slot_amount, dtype=jnp.int32)
    slot_buffer = jnp.max(
        jnp.where(positions[None, :] == slots[:, None], target_slot[None, :], -1), axis=1
    )

    windows = windows.reshape(window_amount, WIN, WIN)
    first, inverse = patches(windows)
    codes, scales = match(
        positions,
        targets * chip_amount + target_slot,
        everyone,
        windows,
        first,
        inverse,
        slot_amount,
    )
    codes = lax.all_to_all(codes, axes, split_axis=0, concat_axis=0, tiled=True)
    notes = jnp.concatenate([scales[:, 0, 0], slot_buffer.astype(jnp.float32)])
    notes = lax.all_gather(notes, axes, axis=0).reshape(devices, 2, devices, capacity)
    notes = lax.dynamic_index_in_dim(notes, lax.axis_index(axes), 2, keepdims=False)
    notes = notes.transpose(0, 2, 1).reshape(slot_amount, 2)
    codes = codes.astype(jnp.float32) * (1.0 / 32767.0)
    scores = (codes * jnp.abs(codes)).reshape(slot_amount, CHIP * CHIP)
    hits_table = (
        notes[None, :, 1] == jnp.arange(chip_amount, dtype=jnp.float32)[:, None]
    ).astype(jnp.float32)
    looks = jnp.sum(hits_table, axis=1)
    share = hits_table * notes[None, :, 0] / jnp.maximum(looks, 1.0)[:, None]
    average = jnp.dot(share, scores, precision=lax.Precision.HIGHEST)
    grid = average.reshape(-1, GC, CHIP * CHIP)
    extended = padded(grid, ((axes, 0),), 1)
    vertical = extended[:-2] + extended[2:]
    sideways = jnp.pad(grid, ((0, 0), (1, 1), (0, 0)))
    horizontal = sideways[:, :-2] + sideways[:, 2:]
    smoothed = (4.0 * grid + vertical + horizontal) / 8.0
    smoothed = smoothed.reshape(chip_amount, half, 2, CHIP)
    return jnp.swapaxes(smoothed, 1, 2).reshape(1, chip_amount, CHIP * CHIP)


def solution(mesh):
    return jax.shard_map(
        on_device,
        mesh=mesh,
        in_specs=(
            P(("groups", "pair"), ("tile", "sub"), None),
            P(("groups", "pair"), ("tile", "sub"), None),
            P(("groups", "pair"), ("tile", "sub"), None),
            P(("groups", "pair"), ("tile", "sub")),
        ),
        out_specs=P(("groups", "pair"), ("tile", "sub"), None),
        check_vma=False,
    )
```

```python
import functools

import jax
import jax.numpy as jnp
from jax import lax
from jax.experimental import pallas as pl
from jax.experimental.pallas import tpu as pltpu
from jax.sharding import PartitionSpec as P

CHIP = 64
WIN = 128
GC = 8
LANES = 128
SUBLANES = 8
PHASES = 4
DEPTH = 80
EACH = 2
SUMMED = 4

epsilon = 1e-06


def padded(block, sides, width):
    for axis, dim in sides:
        count = lax.axis_size(axis)
        forward = [(i, i + 1) for i in range(count - 1)]
        backward = [(target, source) for source, target in forward]
        low = lax.ppermute(
            lax.slice_in_dim(block, block.shape[dim] - width, None, axis=dim), axis, forward
        )
        high = lax.ppermute(lax.slice_in_dim(block, 0, width, axis=dim), axis, backward)
        block = jnp.concatenate([low, block, high], axis=dim)
    return block


def box_sums(image):
    step = 1
    while step < CHIP:
        image = image + pltpu.roll(image, WIN - step, 0)
        step *= 2
    image = image[:CHIP]
    step = 1
    while step < CHIP:
        image = image + pltpu.roll(image, WIN - step, 1)
        step *= 2
    return image


def patch_kernel(windows_ref, first_ref, inverse_ref, copies_ref):
    for item in range(windows_ref.shape[0]):
        window = windows_ref[item].astype(jnp.float32)
        first = box_sums(window)
        second = box_sums(window * window)
        patch_mean = first / (CHIP * CHIP)
        patch_var = second / (CHIP * CHIP) - patch_mean * patch_mean
        for phase in range(PHASES):
            moved = window if phase == 0 else pltpu.roll(window, WIN - phase, 1)
            copies_ref[item, 0, phase] = moved.astype(jnp.bfloat16)
            copies_ref[item, 1, phase] = pltpu.roll(moved, WIN - SUBLANES, 0).astype(jnp.bfloat16)
        first_ref[item] = first
        inverse_ref[item] = 1.0 / (CHIP * jnp.sqrt(patch_var + epsilon))


def patches(windows):
    amount = windows.shape[0]
    surface = jax.ShapeDtypeStruct((amount, CHIP, LANES), jnp.float32)
    block = pl.BlockSpec((SUMMED, CHIP, LANES), lambda i: (i, 0, 0))
    return pl.pallas_call(
        patch_kernel,
        out_shape=(
            surface,
            surface,
            jax.ShapeDtypeStruct((amount, 2, PHASES, WIN, LANES), jnp.bfloat16),
        ),
        grid=(amount // SUMMED,),
        in_specs=[pl.BlockSpec((SUMMED, WIN, WIN), lambda i: (i, 0, 0))],
        out_specs=(
            block,
            block,
            pl.BlockSpec((SUMMED, 2, PHASES, WIN, LANES), lambda i: (i, 0, 0, 0, 0)),
        ),
        compiler_params=pltpu.CompilerParams(vmem_limit_bytes=40 * 1024 * 1024),
        cost_estimate=pl.CostEstimate(
            flops=amount * 2 * 128 * 512 * 256, bytes_accessed=40 * 1024 * 1024, transcendentals=0
        ),
    )(windows)


def correlate(chip_ref, first_ref, inverse_ref, even_ref, odd_ref):
    half = CHIP // 2
    chip = chip_ref[...].astype(jnp.float32)
    total = jnp.sum(jnp.sum(chip, axis=0, keepdims=True), axis=1, keepdims=True)
    mean = total / (CHIP * CHIP)
    centred = chip - mean
    square = jnp.sum(jnp.sum(centred * centred, axis=0, keepdims=True), axis=1, keepdims=True)
    chip_std = jnp.sqrt(square / (CHIP * CHIP) + epsilon)

    lane = lax.broadcasted_iota(jnp.int32, (half, LANES), 1)
    wide = (jnp.where(lane < CHIP, chip, 0.0), jnp.where(lane < CHIP, pltpu.roll(chip, CHIP, 1), 0.0))
    left = []
    for phase in range(PHASES):
        rows = []
        for v in range(phase, CHIP, PHASES):
            row = wide[v // half][v % half : v % half + 1]
            row = jnp.broadcast_to(row, (SUBLANES, LANES))
            rows.append(pltpu.roll(row, 0, 1, stride=1, stride_axis=0))
        left.append(jnp.concatenate(rows, axis=0).astype(jnp.bfloat16)[:, :DEPTH])
    left = jnp.concatenate(left, axis=1)

    groups = CHIP // SUBLANES
    surfaces = []
    for pair in range(groups // 2):
        start = 2 * SUBLANES * pair
        right = jnp.concatenate(
            [
                jnp.concatenate([ref[phase, start : start + DEPTH] for phase in range(PHASES)], axis=0)
                for ref in (even_ref, odd_ref)
            ],
            axis=1,
        )
        partial = jnp.dot(left, right, preferred_element_type=jnp.float32)
        for side in range(2):
            part = partial[:, side * LANES : (side + 1) * LANES]
            value = part[:SUBLANES]
            for far in range(1, CHIP // PHASES):
                rows = part[far * SUBLANES : (far + 1) * SUBLANES]
                value = value + pltpu.roll(rows, LANES - PHASES * far, 1)
            surfaces.append(value)
    raw = jnp.concatenate(surfaces, axis=0)
    return (raw - mean * first_ref[...]) * (inverse_ref[...] / chip_std)


def match_kernel(places_ref, names_ref, *refs):
    chips, rest = refs[:EACH], refs[EACH:]
    copies_ref, first_ref, inverse_ref, out_ref, scale_ref = rest
    step = pl.program_id(0)

    @pl.when(step == 0)
    def _():
        out_ref[...] = jnp.zeros_like(out_ref)
        scale_ref[...] = jnp.zeros_like(scale_ref)

    half = CHIP // 2
    lane = lax.broadcasted_iota(jnp.int32, (half, LANES), 1)
    for item in range(EACH):
        score = correlate(
            chips[item].at[0],
            first_ref.at[item],
            inverse_ref.at[item],
            copies_ref.at[item, 0],
            copies_ref.at[item, 1],
        )
        low, high = score[:half], pltpu.roll(score[half:], CHIP, 1)
        packed = jnp.where(lane < CHIP, low, high)
        size = jnp.abs(packed)
        largest = jnp.max(jnp.max(size, axis=0, keepdims=True), axis=1, keepdims=True)
        largest = jnp.maximum(largest, 1e-30)
        code = jnp.sqrt(size * (1.0 / largest)) * 32767.0
        code = jnp.minimum(code + 0.5, 32767.0).astype(jnp.int32)
        code = jnp.where(packed < 0, -code, code)
        place = places_ref[step * EACH + item]
        out_ref[place] = code.astype(jnp.int16)
        scale_ref[place] = jnp.broadcast_to(largest, (SUBLANES, LANES))


def match(positions, names, everyone, copies, first, inverse, slot_amount):
    amount = copies.shape[0]
    half = CHIP // 2

    def chip_spec(item):
        return pl.BlockSpec((1, half, LANES), lambda i, p, n: (n[i * EACH + item], 0, 0))

    surface = pl.BlockSpec((EACH, CHIP, LANES), lambda i, p, n: (i, 0, 0))
    return pl.pallas_call(
        match_kernel,
        out_shape=(
            jax.ShapeDtypeStruct((slot_amount, half, LANES), jnp.int16),
            jax.ShapeDtypeStruct((slot_amount, SUBLANES, LANES), jnp.float32),
        ),
        grid_spec=pltpu.PrefetchScalarGridSpec(
            num_scalar_prefetch=2,
            grid=(amount // EACH,),
            in_specs=[chip_spec(item) for item in range(EACH)]
            + [
                pl.BlockSpec((EACH, 2, PHASES, WIN, LANES), lambda i, p, n: (i, 0, 0, 0, 0)),
                surface,
                surface,
            ],
            out_specs=(
                pl.BlockSpec((slot_amount, half, LANES), lambda i, p, n: (0, 0, 0)),
                pl.BlockSpec((slot_amount, SUBLANES, LANES), lambda i, p, n: (0, 0, 0)),
            ),
        ),
        compiler_params=pltpu.CompilerParams(vmem_limit_bytes=58 * 1024 * 1024),
        cost_estimate=pl.CostEstimate(
            flops=amount * 2 * 128 * 512 * 1024, bytes_accessed=8 * 1024 * 1024, transcendentals=0
        ),
    )(positions, names, *([everyone] * EACH), copies, first, inverse)


def on_device(ref_chips, search_windows, dest_block, dest_slot):
    axes = ("tile", "sub")
    chips = ref_chips[0]
    windows = search_windows[0]
    targets = dest_block[0, :, 0]
    target_slot = dest_slot[0]
    window_amount = windows.shape[0]
    chip_amount = chips.shape[0]
    half = CHIP // 2
    devices = lax.axis_size(axes)
    capacity = max(2, 2 * window_amount // devices)
    slot_amount = devices * capacity

    turned = jnp.swapaxes(chips.reshape(chip_amount, CHIP, CHIP), 1, 2)
    turned = jnp.swapaxes(turned.reshape(chip_amount, 2, half, CHIP), 1, 2)
    everyone = lax.all_gather(turned.reshape(chip_amount, half, LANES), axes, axis=0, tiled=True)

    order = jnp.arange(window_amount, dtype=jnp.int32)
    matches = targets[:, None] == targets[None, :]
    earlier = order[:, None] > order[None, :]
    ranking = jnp.sum((matches & earlier).astype(jnp.int32), axis=1)
    positions = targets * capacity + ranking
    slots = jnp.arange(slot_amount, dtype=jnp.int32)
    slot_buffer = jnp.max(
        jnp.where(positions[None, :] == slots[:, None], target_slot[None, :], -1), axis=1
    )

    windows = windows.reshape(window_amount, WIN, WIN)
    first, inverse, copies = patches(windows)
    codes, scales = match(
        positions,
        targets * chip_amount + target_slot,
        everyone,
        copies,
        first,
        inverse,
        slot_amount,
    )
    codes = lax.all_to_all(codes, axes, split_axis=0, concat_axis=0, tiled=True)
    notes = jnp.concatenate([scales[:, 0, 0], slot_buffer.astype(jnp.float32)])
    notes = lax.all_gather(notes, axes, axis=0).reshape(devices, 2, devices, capacity)
    notes = lax.dynamic_index_in_dim(notes, lax.axis_index(axes), 2, keepdims=False)
    notes = notes.transpose(0, 2, 1).reshape(slot_amount, 2)
    codes = codes.astype(jnp.float32) * (1.0 / 32767.0)
    scores = (codes * jnp.abs(codes)).reshape(slot_amount, CHIP * CHIP)
    hits_table = (
        notes[None, :, 1] == jnp.arange(chip_amount, dtype=jnp.float32)[:, None]
    ).astype(jnp.float32)
    looks = jnp.sum(hits_table, axis=1)
    share = hits_table * notes[None, :, 0] / jnp.maximum(looks, 1.0)[:, None]
    average = jnp.dot(share, scores, precision=lax.Precision.HIGHEST)
    grid = average.reshape(-1, GC, CHIP * CHIP)
    extended = padded(grid, ((axes, 0),), 1)
    vertical = extended[:-2] + extended[2:]
    sideways = jnp.pad(grid, ((0, 0), (1, 1), (0, 0)))
    horizontal = sideways[:, :-2] + sideways[:, 2:]
    smoothed = (4.0 * grid + vertical + horizontal) / 8.0
    smoothed = smoothed.reshape(chip_amount, half, 2, CHIP)
    return jnp.swapaxes(smoothed, 1, 2).reshape(1, chip_amount, CHIP * CHIP)


def solution(mesh):
    return jax.shard_map(
        on_device,
        mesh=mesh,
        in_specs=(
            P(("groups", "pair"), ("tile", "sub"), None),
            P(("groups", "pair"), ("tile", "sub"), None),
            P(("groups", "pair"), ("tile", "sub"), None),
            P(("groups", "pair"), ("tile", "sub")),
        ),
        out_specs=P(("groups", "pair"), ("tile", "sub"), None),
        check_vma=False,
    )
```

```python
import functools

import jax
import jax.numpy as jnp
from jax import lax
from jax.experimental import pallas as pl
from jax.experimental.pallas import tpu as pltpu
from jax.sharding import PartitionSpec as P

CHIP = 64
WIN = 128
GC = 8
LANES = 128
SUBLANES = 8
PHASES = 8
DEPTH = 80
EACH = 2
SUMMED = 4

epsilon = 1e-06


def padded(block, sides, width):
    for axis, dim in sides:
        count = lax.axis_size(axis)
        forward = [(i, i + 1) for i in range(count - 1)]
        backward = [(target, source) for source, target in forward]
        low = lax.ppermute(
            lax.slice_in_dim(block, block.shape[dim] - width, None, axis=dim), axis, forward
        )
        high = lax.ppermute(lax.slice_in_dim(block, 0, width, axis=dim), axis, backward)
        block = jnp.concatenate([low, block, high], axis=dim)
    return block


def box_sums(image):
    step = 1
    while step < CHIP:
        image = image + pltpu.roll(image, WIN - step, 0)
        step *= 2
    image = image[:CHIP]
    step = 1
    while step < CHIP:
        image = image + pltpu.roll(image, WIN - step, 1)
        step *= 2
    return image


def patch_kernel(windows_ref, first_ref, inverse_ref):
    for item in range(windows_ref.shape[0]):
        window = windows_ref[item].astype(jnp.float32)
        first = box_sums(window)
        second = box_sums(window * window)
        patch_mean = first / (CHIP * CHIP)
        patch_var = second / (CHIP * CHIP) - patch_mean * patch_mean
        first_ref[item] = first
        inverse_ref[item] = 1.0 / (CHIP * jnp.sqrt(patch_var + epsilon))


def patches(windows):
    amount = windows.shape[0]
    surface = jax.ShapeDtypeStruct((amount, CHIP, LANES), jnp.float32)
    block = pl.BlockSpec((SUMMED, CHIP, LANES), lambda i: (i, 0, 0))
    return pl.pallas_call(
        patch_kernel,
        out_shape=(surface, surface),
        grid=(amount // SUMMED,),
        in_specs=[pl.BlockSpec((SUMMED, WIN, WIN), lambda i: (i, 0, 0))],
        out_specs=(block, block),
        cost_estimate=pl.CostEstimate(
            flops=amount * 2 * 128 * 512 * 256, bytes_accessed=40 * 1024 * 1024, transcendentals=0
        ),
    )(windows)


def correlate(chip_ref, window_ref, first_ref, inverse_ref, even_ref, odd_ref):
    half = CHIP // 2
    chip = chip_ref[...].astype(jnp.float32)
    total = jnp.sum(jnp.sum(chip, axis=0, keepdims=True), axis=1, keepdims=True)
    mean = total / (CHIP * CHIP)
    centred = chip - mean
    square = jnp.sum(jnp.sum(centred * centred, axis=0, keepdims=True), axis=1, keepdims=True)
    chip_std = jnp.sqrt(square / (CHIP * CHIP) + epsilon)

    lane = lax.broadcasted_iota(jnp.int32, (half, LANES), 1)
    wide = (jnp.where(lane < CHIP, chip, 0.0), jnp.where(lane < CHIP, pltpu.roll(chip, CHIP, 1), 0.0))
    left = []
    for phase in range(PHASES):
        rows = []
        for v in range(phase, CHIP, PHASES):
            row = wide[v // half][v % half : v % half + 1]
            row = jnp.broadcast_to(row, (SUBLANES, LANES))
            rows.append(pltpu.roll(row, 0, 1, stride=1, stride_axis=0))
        left.append(jnp.concatenate(rows, axis=0).astype(jnp.bfloat16)[:, :DEPTH])
    left = jnp.concatenate(left, axis=1)

    window = window_ref[...].astype(jnp.float32)
    for phase in range(PHASES):
        moved = window if phase == 0 else pltpu.roll(window, WIN - phase, 1)
        even_ref[phase] = moved.astype(jnp.bfloat16)
        odd_ref[phase] = pltpu.roll(moved, WIN - SUBLANES, 0).astype(jnp.bfloat16)

    groups = CHIP // SUBLANES
    surfaces = []
    for pair in range(groups // 2):
        start = 2 * SUBLANES * pair
        right = jnp.concatenate(
            [
                jnp.concatenate([ref[phase, start : start + DEPTH] for phase in range(PHASES)], axis=0)
                for ref in (even_ref, odd_ref)
            ],
            axis=1,
        )
        partial = jnp.dot(left, right, preferred_element_type=jnp.float32)
        for side in range(2):
            part = partial[:, side * LANES : (side + 1) * LANES]
            value = part[:SUBLANES]
            for far in range(1, CHIP // PHASES):
                rows = part[far * SUBLANES : (far + 1) * SUBLANES]
                value = value + pltpu.roll(rows, LANES - PHASES * far, 1)
            surfaces.append(value)
    raw = jnp.concatenate(surfaces, axis=0)
    return (raw - mean * first_ref[...]) * (inverse_ref[...] / chip_std)


def match_kernel(places_ref, names_ref, *refs):
    chips, rest = refs[:EACH], refs[EACH:]
    windows_ref, first_ref, inverse_ref, out_ref, scale_ref, even_ref, odd_ref = rest
    step = pl.program_id(0)

    @pl.when(step == 0)
    def _():
        out_ref[...] = jnp.zeros_like(out_ref)
        scale_ref[...] = jnp.zeros_like(scale_ref)

    half = CHIP // 2
    lane = lax.broadcasted_iota(jnp.int32, (half, LANES), 1)
    for item in range(EACH):
        score = correlate(
            chips[item].at[0],
            windows_ref.at[item],
            first_ref.at[item],
            inverse_ref.at[item],
            even_ref.at[item],
            odd_ref.at[item],
        )
        low, high = score[:half], pltpu.roll(score[half:], CHIP, 1)
        packed = jnp.where(lane < CHIP, low, high)
        size = jnp.abs(packed)
        largest = jnp.max(jnp.max(size, axis=0, keepdims=True), axis=1, keepdims=True)
        largest = jnp.maximum(largest, 1e-30)
        code = jnp.sqrt(size * (1.0 / largest)) * 32767.0
        code = jnp.minimum(code + 0.5, 32767.0).astype(jnp.int32)
        code = jnp.where(packed < 0, -code, code)
        place = places_ref[step * EACH + item]
        out_ref[place] = code.astype(jnp.int16)
        scale_ref[place] = jnp.broadcast_to(largest, (SUBLANES, LANES))


def match(positions, names, everyone, windows, first, inverse, slot_amount):
    amount = windows.shape[0]
    half = CHIP // 2

    def chip_spec(item):
        return pl.BlockSpec((1, half, LANES), lambda i, p, n: (n[i * EACH + item], 0, 0))

    surface = pl.BlockSpec((EACH, CHIP, LANES), lambda i, p, n: (i, 0, 0))
    return pl.pallas_call(
        match_kernel,
        out_shape=(
            jax.ShapeDtypeStruct((slot_amount, half, LANES), jnp.int16),
            jax.ShapeDtypeStruct((slot_amount, SUBLANES, LANES), jnp.float32),
        ),
        grid_spec=pltpu.PrefetchScalarGridSpec(
            num_scalar_prefetch=2,
            grid=(amount // EACH,),
            in_specs=[chip_spec(item) for item in range(EACH)]
            + [pl.BlockSpec((EACH, WIN, WIN), lambda i, p, n: (i, 0, 0)), surface, surface],
            out_specs=(
                pl.BlockSpec((slot_amount, half, LANES), lambda i, p, n: (0, 0, 0)),
                pl.BlockSpec((slot_amount, SUBLANES, LANES), lambda i, p, n: (0, 0, 0)),
            ),
            scratch_shapes=[
                pltpu.VMEM((EACH, PHASES, WIN, LANES), jnp.bfloat16),
                pltpu.VMEM((EACH, PHASES, WIN, LANES), jnp.bfloat16),
            ],
        ),
        compiler_params=pltpu.CompilerParams(vmem_limit_bytes=58 * 1024 * 1024),
        cost_estimate=pl.CostEstimate(
            flops=amount * 2 * 128 * 512 * 1024, bytes_accessed=8 * 1024 * 1024, transcendentals=0
        ),
    )(positions, names, *([everyone] * EACH), windows, first, inverse)


def on_device(ref_chips, search_windows, dest_block, dest_slot):
    axes = ("tile", "sub")
    chips = ref_chips[0]
    windows = search_windows[0]
    targets = dest_block[0, :, 0]
    target_slot = dest_slot[0]
    window_amount = windows.shape[0]
    chip_amount = chips.shape[0]
    half = CHIP // 2
    devices = lax.axis_size(axes)
    capacity = max(2, 2 * window_amount // devices)
    slot_amount = devices * capacity

    turned = jnp.swapaxes(chips.reshape(chip_amount, CHIP, CHIP), 1, 2)
    turned = jnp.swapaxes(turned.reshape(chip_amount, 2, half, CHIP), 1, 2)
    everyone = lax.all_gather(turned.reshape(chip_amount, half, LANES), axes, axis=0, tiled=True)

    order = jnp.arange(window_amount, dtype=jnp.int32)
    matches = targets[:, None] == targets[None, :]
    earlier = order[:, None] > order[None, :]
    ranking = jnp.sum((matches & earlier).astype(jnp.int32), axis=1)
    positions = targets * capacity + ranking
    slots = jnp.arange(slot_amount, dtype=jnp.int32)
    slot_buffer = jnp.max(
        jnp.where(positions[None, :] == slots[:, None], target_slot[None, :], -1), axis=1
    )

    windows = windows.reshape(window_amount, WIN, WIN)
    first, inverse = patches(windows)
    codes, scales = match(
        positions,
        targets * chip_amount + target_slot,
        everyone,
        windows,
        first,
        inverse,
        slot_amount,
    )
    codes = lax.all_to_all(codes, axes, split_axis=0, concat_axis=0, tiled=True)
    notes = jnp.concatenate([scales[:, 0, 0], slot_buffer.astype(jnp.float32)])
    notes = lax.all_gather(notes, axes, axis=0).reshape(devices, 2, devices, capacity)
    notes = lax.dynamic_index_in_dim(notes, lax.axis_index(axes), 2, keepdims=False)
    notes = notes.transpose(0, 2, 1).reshape(slot_amount, 2)
    codes = codes.astype(jnp.float32) * (1.0 / 32767.0)
    scores = (codes * jnp.abs(codes)).reshape(slot_amount, CHIP * CHIP)
    hits_table = (
        notes[None, :, 1] == jnp.arange(chip_amount, dtype=jnp.float32)[:, None]
    ).astype(jnp.float32)
    looks = jnp.sum(hits_table, axis=1)
    share = hits_table * notes[None, :, 0] / jnp.maximum(looks, 1.0)[:, None]
    average = jnp.dot(share, scores, precision=lax.Precision.HIGHEST)
    grid = average.reshape(-1, GC, CHIP * CHIP)
    extended = padded(grid, ((axes, 0),), 1)
    vertical = extended[:-2] + extended[2:]
    sideways = jnp.pad(grid, ((0, 0), (1, 1), (0, 0)))
    horizontal = sideways[:, :-2] + sideways[:, 2:]
    smoothed = (4.0 * grid + vertical + horizontal) / 8.0
    smoothed = smoothed.reshape(chip_amount, half, 2, CHIP)
    return jnp.swapaxes(smoothed, 1, 2).reshape(1, chip_amount, CHIP * CHIP)


def solution(mesh):
    return jax.shard_map(
        on_device,
        mesh=mesh,
        in_specs=(
            P(("groups", "pair"), ("tile", "sub"), None),
            P(("groups", "pair"), ("tile", "sub"), None),
            P(("groups", "pair"), ("tile", "sub"), None),
            P(("groups", "pair"), ("tile", "sub")),
        ),
        out_specs=P(("groups", "pair"), ("tile", "sub"), None),
        check_vma=False,
    )
```
